32 devices in a mesh: grp: 2 (over x), col: 8 (over z, y), row: 2 (over core).
Axes of the slice: x: 2, y: 2, z: 4, core: 2. Of those that a mesh axis runs over, the one named last changes fastest.
Arguments:
- grad_out: bfloat16 [384, 8192], P('grp', 'col'), parts along dimension 0, may hold values from -6 to 6
- hidden: bfloat16 [384, 26624], P(('grp', 'col'), 'row'), parts along dimension 0, may hold values from -6 to 6
- weight: bfloat16 [8192, 26624], P('col', 'row'), may hold values from -0.0625 to 0.0625
- proj_in: bfloat16 [64, 26624], P(None, 'row'), may hold values from -0.0390625 to 0.0390625
- proj_out: bfloat16 [64, 8192], P(None, 'col'), may hold values from -0.0625 to 0.0625
- doc_len: int32 [32], P('grp'), parts along dimension 0, may hold values from 1 to 48, 192 in all
Outputs:
- input_grad: bfloat16 [384, 26624], P(('grp', 'col'), 'row'), parts along dimension 0
- doc_grads: float32 [32, 64, 64], P('grp'), parts along dimension 0
The draws below stay inside these ranges and needn't reach their ends.
There are 2 independent parts, one for each index of `grp`. The reference program is written for one: setup_inputs(seed, part) draws one part's arguments, and reference() takes and returns one part's arrays. A program takes and returns all parts, laid end to end along the dimension named above; an argument that names none is the same for every part. Nothing has to cross between parts.
Inputs may be any that keep to these rules, and one draw needn't show every extreme that they name: doc_len sums to 192; its largest entry is exactly 48.
All inputs are finite; a program needn't handle non-finite values.
Results may differ from the reference program's by a relative error of at most 0.014.
Values may be sent and summed in bfloat16 or wider, within the bound.
A program may use at most 128 MiB of HBM per device.

```python
import math
import jax
import jax.numpy as jnp
import numpy as np
from jax import lax

D = 8192
FF = 26624
KR = 64
DOCS = 16
TOKENS = 192
MOST = 48
N_COL = 8


def with_spikes(values, stream_key, source, target, shards_of, factor):
    owner, partner = [(jnp.arange(values.shape[axis_at]) // (values.shape[axis_at] // shards_of)).reshape([-1 if axis == axis_at else 1 for axis in range(values.ndim)]) for axis_at in (source, target)]
    chosen = jax.random.permutation(stream_key, shards_of)[partner]
    strong = (owner == chosen) | (owner == (partner + shards_of // 2) % shards_of)
    return jnp.where(strong, factor * values, values)


def block_levels(own_key, shape, shards, least, top_value):
    level, own = 1.0, jax.random.fold_in(own_key, 6)
    for dim, parts in shards:
        draws = jnp.exp(jax.random.uniform(jax.random.fold_in(own, dim), (parts,), jnp.float32, least / len(shards), top_value / len(shards)))
        level = level * jnp.repeat(draws, shape[dim] // parts).reshape([-1 if axis == dim else 1 for axis in range(len(shape))])
    return level


def profile(number_of, total, bound, lean):
    weights = [(1 << 20) // math.isqrt(rank ** lean) + 1 for rank in range(2, number_of + 1)]
    surplus, holding = total - bound - (number_of - 1), [1] * (number_of - 1)
    while surplus > 0:
        movable = [i for i in range(number_of - 1) if holding[i] < bound]
        mass, left = sum([weights[i] for i in movable]), surplus
        for i in movable:
            extra = min(bound - holding[i], max(1, left * weights[i] // mass), surplus)
            holding[i] = holding[i] + extra
            surplus = surplus - extra
    return np.array([bound] + holding)


def uneven_parts(stream_key, number_of, total, bound, skew):
    if number_of == 2:
        one = jax.random.randint(stream_key, (), max(1, total - bound), min(bound, total - 1) + 1)
        return jnp.stack([one, total - one])
    tallies = jnp.asarray(profile(number_of, total, bound, skew), jnp.int32)
    pairs = (number_of - 1) // 2
    giver, receiver = tallies[1:1 + 2 * pairs:2], tallies[2:2 + 2 * pairs:2]
    slack = jnp.minimum(giver - 1, bound - receiver)
    passed = jax.random.randint(jax.random.fold_in(stream_key, 1), (pairs,), 0, 1 << 20) % (slack + 1)
    tallies = tallies.at[1:1 + 2 * pairs:2].set(giver - passed).at[2:2 + 2 * pairs:2].set(receiver + passed)
    return tallies[jax.random.permutation(jax.random.fold_in(stream_key, 2), number_of)]


def centred(rng, dims, spread, most, cuts=(), held_as=jnp.bfloat16):
    drawn = jax.random.normal(rng, dims, jnp.float32) * spread
    if len(cuts) > 0:
        drawn = block_levels(rng, dims, cuts, -0.22, 0.18) * drawn
    return jnp.clip(drawn, min=-most, max=most).astype(held_as)


def gaussian_with(stream_key, extent, scale, reach, cuts, heavy, kind=jnp.bfloat16):
    values = scale * jax.random.normal(stream_key, extent, jnp.float32)
    if cuts:
        values = values * block_levels(stream_key, extent, cuts, -0.22, 0.18)
    return jnp.clip(with_spikes(values, jax.random.fold_in(stream_key, 3), *heavy), -reach, reach).astype(kind)


def setup_inputs(seed: int = 0, part: int = 0) -> dict:
    key_list = jax.random.split(jax.random.key(seed), 7)
    part_keys = jax.random.split(jax.random.fold_in(key_list[6], part), 7)
    grad_out = gaussian_with(part_keys[0], (TOKENS, D), 1.0, 6.0, ((1, 8),), (1, 0, 8, 2.0))
    hidden = centred(part_keys[1], (TOKENS, FF), 1.0, 6.0, ((0, 8), (1, 2)))
    weight = centred(key_list[2], (D, FF), D ** -0.5, 0.0625, ((0, 8), (1, 2)))
    proj_in = centred(key_list[3], (KR, FF), FF ** -0.5, 0.0390625, ((1, 2),))
    proj_out = centred(key_list[4], (KR, D), D ** -0.5, 0.0625, ((1, 8),))
    doc_len = uneven_parts(part_keys[5], DOCS, TOKENS, MOST, 2).astype(jnp.int32)
    return dict(grad_out=grad_out, hidden=hidden, weight=weight, proj_in=proj_in, proj_out=proj_out, doc_len=doc_len)


def reference(grad_out, hidden, weight, proj_in, proj_out, doc_len):
    width = D // N_COL
    contract = (((1,), (1,)), ((), ()))

    def add_block(carry, block):
        offset = block * width
        cot_rows = lax.dynamic_slice_in_dim(grad_out, offset, width, 1)
        weight_rows = lax.dynamic_slice_in_dim(weight, offset, width, 0)
        proj_rows = lax.dynamic_slice_in_dim(proj_out, offset, width, 1)
        partial_grad = jnp.dot(cot_rows, weight_rows, preferred_element_type=jnp.float32).astype(jnp.bfloat16)
        partial_sketch = lax.dot_general(cot_rows, proj_rows, contract, preferred_element_type=jnp.float32).astype(jnp.bfloat16)
        return (carry[0] + partial_grad.astype(jnp.float32), carry[1] + partial_sketch.astype(jnp.float32)), None

    start_carry = (jnp.zeros((TOKENS, FF), jnp.float32), jnp.zeros((TOKENS, KR), jnp.float32))
    totals, _ = lax.scan(add_block, start_carry, jnp.arange(N_COL, dtype=jnp.int32))
    input_grad = totals[0].astype(jnp.bfloat16)
    out_sketch = totals[1].astype(jnp.bfloat16)
    in_sketch = lax.dot_general(hidden, proj_in, contract, preferred_element_type=jnp.float32).astype(jnp.bfloat16)
    starts = (jnp.cumsum(doc_len) - doc_len).astype(jnp.int32)
    places = jnp.arange(TOKENS, dtype=jnp.int32)
    member = (places[None, :] >= starts[:, None]) & (places[None, :] < (starts + doc_len)[:, None])
    weighted = member.astype(jnp.float32)[:, :, None] * out_sketch.astype(jnp.float32)[None, :, :]
    doc_grads = jnp.einsum("sti,tj->sij", weighted, in_sketch.astype(jnp.float32))
    return input_grad, doc_grads
```

```python
import functools

import jax
import jax.numpy as jnp
from jax import lax
from jax.experimental import pallas as pl
from jax.experimental.pallas import tpu as pltpu
from jax.sharding import PartitionSpec as P

MESH = pl.DeviceIdType.MESH
F32, BF16 = jnp.float32, jnp.bfloat16
NT_DIMS = (((1,), (1,)), ((), ()))


def member_table(doc_len, first, count):
    starts = jnp.cumsum(doc_len) - doc_len
    places = first + jnp.arange(count, dtype=jnp.int32)
    member = (places[None, :] >= starts[:, None]) & (places[None, :] < (starts + doc_len)[:, None])
    return member.astype(jnp.float32)


def doc_terms(doc_len, first, out_part, in_part):
    member = member_table(doc_len, first, out_part.shape[0])
    weighted = member[:, :, None] * out_part.astype(jnp.float32)[None, :, :]
    return jnp.einsum("sti,tj->sij", weighted, in_part.astype(jnp.float32))


def local(grad_out, hidden, weight, proj_in, proj_out, doc_len):
    contract = (((1,), (1,)), ((), ()))
    local_rows = hidden.shape[0]
    local_in = lax.dot_general(hidden, proj_in, contract, preferred_element_type=jnp.float32)
    in_sketch = lax.psum(local_in, "row").astype(jnp.bfloat16)
    input_grad = lax.psum_scatter(
        jnp.dot(grad_out, weight, preferred_element_type=jnp.float32).astype(jnp.bfloat16),
        "col",
        scatter_dimension=0,
        tiled=True,
    )
    local_out = lax.dot_general(grad_out, proj_out, contract, preferred_element_type=jnp.float32)
    out_sketch = lax.psum_scatter(
        local_out.astype(jnp.bfloat16), "col", scatter_dimension=0, tiled=True
    )
    first = lax.axis_index("col") * local_rows
    local_docs = doc_terms(doc_len, first, out_sketch, in_sketch)
    doc_grads = lax.psum(local_docs.astype(jnp.bfloat16), "col").astype(jnp.float32)
    return (input_grad, doc_grads)


def add(a, b):
    return (a.astype(F32) + b.astype(F32)).astype(BF16)


def kernel(
    T, nt, nzt, wbufs,
    doc_ref, grad_hbm, hid_hbm, w_hbm, pin_hbm, pout_hbm,
    og_ref, docs_ref,
    gp, gf, gb, hid, pin, pout, wb,
    S, Q, YR, RR, RL, FO, FS, FR,
    SK, SKR, ISK, ISR, G,
    ld_sem, w_sem,
    y_s, y_r, zr_s, zr_r, zl_s, zl_r, f_s, f_r,
    sk_s, sk_r, is_sem, g_s, g_r,
):
    nz, ny = 2 * nzt, nt - nzt
    nu = nz + ny
    half = T // 2
    rows = gp.shape[1]
    kr = pout.shape[0]
    ff = hid.shape[1]

    c = lax.axis_index("col")
    r = lax.axis_index("row")
    y, z = lax.rem(c, 2), lax.div(c, 2)
    other = c + 1 - 2 * y
    right, left = lax.rem(c + 2, 8), lax.rem(c + 6, 8)

    def dest(i):
        return 2 * (i % 4) + (y if i < 4 else 1 - y)

    grad_in = [pltpu.make_async_copy(grad_hbm.at[dest(i)], gp.at[i], ld_sem.at[i]) for i in range(8)]
    for cp in grad_in:
        cp.start()

    def w_copy(t):
        return pltpu.make_async_copy(
            w_hbm.at[:, pl.ds(pl.multiple_of(t * T, T), T)], wb.at[lax.rem(t, wbufs)], w_sem.at[lax.rem(t, wbufs)]
        )

    w_copy(jnp.int32(0)).start()
    pout_in = pltpu.make_async_copy(pout_hbm, pout, ld_sem.at[8])
    pin_in = pltpu.make_async_copy(pin_hbm, pin, ld_sem.at[9])
    hid_in = pltpu.make_async_copy(hid_hbm, hid, ld_sem.at[10])
    for t in range(1, wbufs):
        w_copy(jnp.int32(t)).start()
    pout_in.start()
    hid_in.start()
    pin_in.start()

    barrier = pltpu.get_barrier_semaphore()
    for d in range(1, 8):
        pl.semaphore_signal(barrier, inc=1, device_id={"col": lax.rem(c + d, 8)}, device_id_type=MESH)
    pl.semaphore_signal(barrier, inc=1, device_id={"row": 1 - r}, device_id_type=MESH)

    def remote(src, dst, s, rcv, to):
        return pltpu.make_async_remote_copy(
            src_ref=src, dst_ref=dst, send_sem=s, recv_sem=rcv, device_id=to, device_id_type=MESH
        )

    def y_copy(k):
        return remote(Q.at[k], YR.at[k], y_s.at[k], y_r.at[k], {"col": other})

    def zr_copy(u, lo):
        return remote(S.at[u, lo:4], RR.at[u, lo - 1 : 3], zr_s.at[u], zr_r.at[u], {"col": right})

    def zl_copy(u, hi):
        return remote(S.at[u, 0:hi], RL.at[u, 0:hi], zl_s.at[u], zl_r.at[u], {"col": left})

    def f_copy(u):
        return remote(FS.at[u], FR.at[u], f_s.at[u], f_r.at[u], {"col": other})

    def end_sends(u):
        @pl.when(z == 0)
        def _():
            zr_copy(u, 1).start()

        @pl.when(z == 3)
        def _():
            zl_copy(u, 3).start()

    for cp in grad_in:
        cp.wait()
    for i in range(8):
        gf[rows * i : rows * (i + 1), :] = gp[i].astype(F32)
    gb[...] = gf[...].astype(BF16)

    def product(slot, at):
        return jnp.dot(gb[...], wb[slot, :, at : at + half], preferred_element_type=F32)

    def refill(t):
        @pl.when(t + wbufs < nt)
        def _():
            w_copy(t + wbufs).start()

    def y_tile(t):
        k = jnp.where(t == 0, 0, t - nzt)
        w_copy(t).wait()
        slot = lax.rem(t, wbufs)
        for n in range(2):
            got = product(slot, n * half)
            for b in range(4):
                S[nz + k, b, :, n * half : (n + 1) * half] = got[rows * b : rows * (b + 1)].astype(BF16)
                Q[k, b, :, n * half : (n + 1) * half] = got[rows * (b + 4) : rows * (b + 5)].astype(BF16)
        refill(t)
        y_copy(k).start()

    def z_tile(t):
        w_copy(t).wait()
        slot = lax.rem(t, wbufs)
        for n in range(2):
            u = 2 * (t - 1) + n
            got = product(slot, n * half)
            for b in range(4):
                S[u, b, :, 0:half] = got[rows * b : rows * (b + 1)].astype(BF16)
                S[u, b, :, half:T] = got[rows * (b + 4) : rows * (b + 5)].astype(BF16)
            end_sends(u)
        refill(t)

    def over(first, last, body):
        def step(i, carry):
            body(i)
            return carry

        lax.fori_loop(first, last, step, 0)

    pl.semaphore_wait(barrier, 8)

    over(0, 1, y_tile)
    over(1, 1 + nzt, z_tile)

    def sk_copy(i):
        return remote(SK.at[i], SKR.at[c], sk_s.at[i], sk_r.at[c], {"col": dest(i)})

    def sk_arrival(j):
        return remote(SK.at[0], SKR.at[j], sk_s.at[0], sk_r.at[j], {"col": other})

    is_copy = remote(ISK, ISR, is_sem.at[0], is_sem.at[1], {"row": 1 - r})

    def g_copy(d):
        return remote(G.at[c], G.at[c], g_s.at[d - 1], g_r.at[c], {"col": lax.rem(c + d, 8)})

    def g_arrival(j):
        return remote(G.at[j], G.at[j], g_s.at[0], g_r.at[j], {"col": other})

    pout_in.wait()
    sketch = lax.dot_general(gb[...], pout[...], NT_DIMS, preferred_element_type=F32)
    blank = jnp.zeros((rows, 128 - kr), F32)
    for i in range(8):
        SK[i] = jnp.concatenate([sketch[rows * i : rows * (i + 1)], blank], axis=1).astype(BF16)
        if i < 4:
            @pl.when(z != i)
            def _():
                sk_copy(i).start()
        else:
            sk_copy(i).start()
    hid_in.wait()
    pin_in.wait()
    part = jnp.zeros((rows, kr), F32)
    for k in range(ff // T):
        part += lax.dot_general(
            hid[:, k * T : (k + 1) * T], pin[:, k * T : (k + 1) * T], NT_DIMS, preferred_element_type=F32
        )
    ISK[...] = jnp.concatenate([blank, part], axis=1)
    is_copy.start()

    over(1 + nzt, nt, y_tile)

    total = SK[z].astype(F32)
    for d in range(1, 8):
        j = lax.rem(c + d, 8)
        sk_arrival(j).wait_recv()
        total += SKR[j].astype(F32)
    is_copy.wait_recv()
    G[c] = (total + (ISK[...] + ISR[...])).astype(BF16)
    for d in range(1, 8):
        g_copy(d).start()

    def y_stage(u):
        k = u - nz
        y_copy(k).wait_recv()
        for b in range(4):
            S[u, b] = add(S[u, b], YR[k, b])
        end_sends(u)

    def second(u):
        @pl.when(z == 1)
        def _():
            zr_copy(u, 1).wait_recv()
            for b in (2, 3):
                S[u, b] = add(S[u, b], RR[u, b - 1])
            zr_copy(u, 2).start()

        @pl.when(z == 2)
        def _():
            zl_copy(u, 3).wait_recv()
            for b in (0, 1):
                S[u, b] = add(S[u, b], RL[u, b])
            zl_copy(u, 2).start()

    def third(u):
        @pl.when(z == 2)
        def _():
            zr_copy(u, 2).wait_recv()
            S[u, 3] = add(S[u, 3], RR[u, 2])
            zr_copy(u, 3).start()

        @pl.when(z == 1)
        def _():
            zl_copy(u, 2).wait_recv()
            S[u, 0] = add(S[u, 0], RL[u, 0])
            zl_copy(u, 1).start()

    def store(u, value):
        @pl.when(u < nz)
        def _():
            FO[u] = value[:, 0:half].astype(BF16)
            FS[u] = value[:, half:T].astype(BF16)
            f_copy(u).start()

        @pl.when(u >= nz)
        def _():
            k = u - nz
            t = jnp.where(k == 0, 0, k + nzt)
            og_ref[:, pl.ds(pl.multiple_of(t * T, T), T)] = value.astype(BF16)

    def last(u):
        @pl.when(z == 0)
        def _():
            zl_copy(u, 1).wait_recv()
            store(u, S[u, 0].astype(F32) + RL[u, 0].astype(F32))

        @pl.when(z == 3)
        def _():
            zr_copy(u, 3).wait_recv()
            store(u, S[u, 3].astype(F32) + RR[u, 2].astype(F32))

        @pl.when(z == 1)
        def _():
            store(u, S[u, 1].astype(F32) + RR[u, 0].astype(F32) + RL[u, 1].astype(F32))

        @pl.when(z == 2)
        def _():
            store(u, S[u, 2].astype(F32) + RR[u, 1].astype(F32) + RL[u, 2].astype(F32))

    def fold(u):
        f_copy(u).wait_recv()
        og_ref[:, pl.ds(pl.multiple_of(T + u * half, half), half)] = add(FO[u], FR[u])

    def step(i):
        @pl.when((i >= nz) & (i < nu))
        def _():
            y_stage(i)

        @pl.when((i >= 1) & (i < nu + 1))
        def _():
            second(i - 1)

        @pl.when((i >= 2) & (i < nu + 2))
        def _():
            third(i - 2)

        @pl.when((i >= 3) & (i < nu + 3))
        def _():
            last(i - 3)

        @pl.when((i >= 5) & (i < nz + 5))
        def _():
            fold(i - 5)

    over(0, nz + 5, step)

    for d in range(1, 8):
        g_arrival(lax.rem(c + d, 8)).wait_recv()
    both = jnp.concatenate([G[j].astype(F32) for j in range(8)], axis=0).astype(BF16)
    eye = (
        lax.broadcasted_iota(jnp.int32, (kr, 128), 0) == lax.broadcasted_iota(jnp.int32, (kr, 128), 1)
    ).astype(F32).astype(BF16)
    turned = lax.dot_general(eye, both, NT_DIMS, preferred_element_type=F32)
    place = lax.broadcasted_iota(jnp.int32, turned.shape, 1)
    start = jnp.int32(0)
    for s in range(docs_ref.shape[0]):
        stop = start + doc_ref[s]
        mine = jnp.where((place >= start) & (place < stop), turned, 0.0).astype(BF16)
        docs_ref[s] = jnp.dot(mine, both, preferred_element_type=F32)[:, kr : 2 * kr]
        start = stop

    over(nz + 5, nu + 3, step)

    def sent_y(k):
        y_copy(k).wait_send()

    def sent_f(u):
        f_copy(u).wait_send()

    def sent_z(u):
        for at in range(4):
            @pl.when(z == at)
            def _():
                if at < 3:
                    zr_copy(u, at + 1).wait_send()
                if at > 0:
                    zl_copy(u, at).wait_send()

    over(0, ny, sent_y)
    over(0, nz, sent_f)
    over(0, nu, sent_z)
    for i in range(8):
        if i < 4:
            @pl.when(z != i)
            def _():
                sk_copy(i).wait_send()
        else:
            sk_copy(i).wait_send()
    is_copy.wait_send()
    for d in range(1, 8):
        g_copy(d).wait_send()


def fused(grad_out, hidden, weight, proj_in, proj_out, doc_len, T=512, wbufs=4):
    tokens, depth = grad_out.shape
    rows, ff = hidden.shape
    kr = proj_in.shape[0]
    docs = doc_len.shape[0]
    nt = ff // T
    nzt = max(1, (2 * nt + 6) // 13)
    nz, ny = 2 * nzt, nt - nzt
    nu = nz + ny
    dma = pltpu.SemaphoreType.DMA
    any_spec = pl.BlockSpec(memory_space=pl.ANY)
    vmem_spec = pl.BlockSpec(memory_space=pltpu.VMEM)
    return pl.pallas_call(
        functools.partial(kernel, T, nt, nzt, wbufs),
        out_shape=(
            jax.ShapeDtypeStruct((rows, ff), BF16),
            jax.ShapeDtypeStruct((docs, kr, kr), F32),
        ),
        in_specs=[pl.BlockSpec(memory_space=pltpu.SMEM)] + [any_spec] * 5,
        out_specs=(vmem_spec, vmem_spec),
        scratch_shapes=[
            pltpu.VMEM((8, rows, depth), BF16),
            pltpu.VMEM((tokens, depth), F32),
            pltpu.VMEM((tokens, depth), BF16),
            pltpu.VMEM((rows, ff), BF16),
            pltpu.VMEM((kr, ff), BF16),
            pltpu.VMEM((kr, depth), BF16),
            pltpu.VMEM((wbufs, depth, T), BF16),
            pltpu.VMEM((nu, 4, rows, T), BF16),
            pltpu.VMEM((ny, 4, rows, T), BF16),
            pltpu.VMEM((ny, 4, rows, T), BF16),
            pltpu.VMEM((nu, 3, rows, T), BF16),
            pltpu.VMEM((nu, 3, rows, T), BF16),
            pltpu.VMEM((nz, rows, T // 2), BF16),
            pltpu.VMEM((nz, rows, T // 2), BF16),
            pltpu.VMEM((nz, rows, T // 2), BF16),
            pltpu.VMEM((8, rows, 128), BF16),
            pltpu.VMEM((8, rows, 128), BF16),
            pltpu.VMEM((rows, 128), F32),
            pltpu.VMEM((rows, 128), F32),
            pltpu.VMEM((8, rows, 128), BF16),
            dma((11,)),
            dma((wbufs,)),
            dma((ny,)), dma((ny,)),
            dma((nu,)), dma((nu,)), dma((nu,)), dma((nu,)),
            dma((nz,)), dma((nz,)),
            dma((8,)), dma((8,)), dma((2,)), dma((7,)), dma((8,)),
        ],
        compiler_params=pltpu.CompilerParams(
            collective_id=0, has_side_effects=True, vmem_limit_bytes=48 * 1024 * 1024
        ),
        cost_estimate=pl.CostEstimate(
            flops=2 * tokens * depth * ff, bytes_accessed=2 * depth * ff, transcendentals=0
        ),
    )(doc_len, grad_out.reshape(8, rows, depth), hidden, weight, proj_in, proj_out)


def solution(mesh):
    in_specs = (
        P("grp", "col"),
        P(("grp", "col"), "row"),
        P("col", "row"),
        P(None, "row"),
        P(None, "col"),
        P("grp"),
    )
    out_specs = (P(("grp", "col"), "row"), P("grp", None, None))
    body = fused if mesh.shape["col"] == 8 and mesh.shape["row"] == 2 else local
    return jax.shard_map(body, mesh=mesh, in_specs=in_specs, out_specs=out_specs, check_vma=False)
```

```python
import functools

import jax
import jax.numpy as jnp
from jax import lax
from jax.experimental import pallas as pl
from jax.experimental.pallas import tpu as pltpu
from jax.sharding import PartitionSpec as P

MESH = pl.DeviceIdType.MESH
F32, BF16 = jnp.float32, jnp.bfloat16
NT_DIMS = (((1,), (1,)), ((), ()))


def member_table(doc_len, first, count):
    starts = jnp.cumsum(doc_len) - doc_len
    places = first + jnp.arange(count, dtype=jnp.int32)
    member = (places[None, :] >= starts[:, None]) & (places[None, :] < (starts + doc_len)[:, None])
    return member.astype(jnp.float32)


def doc_terms(doc_len, first, out_part, in_part):
    member = member_table(doc_len, first, out_part.shape[0])
    weighted = member[:, :, None] * out_part.astype(jnp.float32)[None, :, :]
    return jnp.einsum("sti,tj->sij", weighted, in_part.astype(jnp.float32))


def local(grad_out, hidden, weight, proj_in, proj_out, doc_len):
    contract = (((1,), (1,)), ((), ()))
    local_rows = hidden.shape[0]
    local_in = lax.dot_general(hidden, proj_in, contract, preferred_element_type=jnp.float32)
    in_sketch = lax.psum(local_in, "row").astype(jnp.bfloat16)
    input_grad = lax.psum_scatter(
        jnp.dot(grad_out, weight, preferred_element_type=jnp.float32).astype(jnp.bfloat16),
        "col",
        scatter_dimension=0,
        tiled=True,
    )
    local_out = lax.dot_general(grad_out, proj_out, contract, preferred_element_type=jnp.float32)
    out_sketch = lax.psum_scatter(
        local_out.astype(jnp.bfloat16), "col", scatter_dimension=0, tiled=True
    )
    first = lax.axis_index("col") * local_rows
    local_docs = doc_terms(doc_len, first, out_sketch, in_sketch)
    doc_grads = lax.psum(local_docs.astype(jnp.bfloat16), "col").astype(jnp.float32)
    return (input_grad, doc_grads)


def add(a, b):
    return (a.astype(F32) + b.astype(F32)).astype(BF16)


def kernel(
    T, nt, nzt, wbufs, lag,
    doc_ref, grad_hbm, hid_hbm, w_hbm, pin_hbm, pout_hbm,
    og_ref, docs_ref,
    gp, gf, gb, hid, pin, pout, wb,
    S, Q, YR, RR, RL, FO, FS, FR,
    SK, SKR, ISK, ISR, G,
    ld_sem, w_sem,
    y_s, y_r, zr_s, zr_r, zl_s, zl_r, f_s, f_r,
    sk_s, sk_r, is_sem, g_s, g_r,
):
    nz, ny = 2 * nzt, nt - nzt
    nu = nz + ny
    early = min(3 + nzt, nt)
    half = T // 2
    rows = gp.shape[1]
    kr = pout.shape[0]
    ff = hid.shape[1]

    c = lax.axis_index("col")
    r = lax.axis_index("row")
    y, z = lax.rem(c, 2), lax.div(c, 2)
    other = c + 1 - 2 * y
    right, left = lax.rem(c + 2, 8), lax.rem(c + 6, 8)

    def dest(i):
        return 2 * (i % 4) + (y if i < 4 else 1 - y)

    grad_in = [pltpu.make_async_copy(grad_hbm.at[dest(i)], gp.at[i], ld_sem.at[i]) for i in range(8)]
    for cp in grad_in:
        cp.start()

    def w_copy(t):
        return pltpu.make_async_copy(
            w_hbm.at[:, pl.ds(pl.multiple_of(t * T, T), T)], wb.at[lax.rem(t, wbufs)], w_sem.at[lax.rem(t, wbufs)]
        )

    w_copy(jnp.int32(0)).start()
    pout_in = pltpu.make_async_copy(pout_hbm, pout, ld_sem.at[8])
    pin_in = pltpu.make_async_copy(pin_hbm, pin, ld_sem.at[9])
    hid_in = pltpu.make_async_copy(hid_hbm, hid, ld_sem.at[10])
    for t in range(1, wbufs):
        w_copy(jnp.int32(t)).start()
    pout_in.start()
    hid_in.start()
    pin_in.start()

    barrier = pltpu.get_barrier_semaphore()
    for d in range(1, 8):
        pl.semaphore_signal(barrier, inc=1, device_id={"col": lax.rem(c + d, 8)}, device_id_type=MESH)
    pl.semaphore_signal(barrier, inc=1, device_id={"row": 1 - r}, device_id_type=MESH)

    def remote(src, dst, s, rcv, to):
        return pltpu.make_async_remote_copy(
            src_ref=src, dst_ref=dst, send_sem=s, recv_sem=rcv, device_id=to, device_id_type=MESH
        )

    def y_copy(k):
        return remote(Q.at[k], YR.at[k], y_s.at[k], y_r.at[k], {"col": other})

    def zr_copy(u, lo):
        return remote(S.at[u, lo:4], RR.at[u, lo - 1 : 3], zr_s.at[u], zr_r.at[u], {"col": right})

    def zl_copy(u, hi):
        return remote(S.at[u, 0:hi], RL.at[u, 0:hi], zl_s.at[u], zl_r.at[u], {"col": left})

    def f_copy(u):
        return remote(FS.at[u], FR.at[u], f_s.at[u], f_r.at[u], {"col": other})

    def end_sends(u):
        @pl.when(z == 0)
        def _():
            zr_copy(u, 1).start()

        @pl.when(z == 3)
        def _():
            zl_copy(u, 3).start()

    for cp in grad_in:
        cp.wait()
    for i in range(8):
        gf[rows * i : rows * (i + 1), :] = gp[i].astype(F32)
    gb[...] = gf[...].astype(BF16)

    def product(slot, at):
        return jnp.dot(gb[...], wb[slot, :, at : at + half], preferred_element_type=F32)

    def refill(t):
        @pl.when(t + wbufs < nt)
        def _():
            w_copy(t + wbufs).start()

    def y_tile(t):
        k = jnp.where(t == 0, 0, t - nzt)
        w_copy(t).wait()
        slot = lax.rem(t, wbufs)
        for n in range(2):
            got = product(slot, n * half)
            for b in range(4):
                S[nz + k, b, :, n * half : (n + 1) * half] = got[rows * b : rows * (b + 1)].astype(BF16)
                Q[k, b, :, n * half : (n + 1) * half] = got[rows * (b + 4) : rows * (b + 5)].astype(BF16)
        refill(t)
        y_copy(k).start()

    def z_tile(t):
        w_copy(t).wait()
        slot = lax.rem(t, wbufs)
        for n in range(2):
            u = 2 * (t - 1) + n
            got = product(slot, n * half)
            for b in range(4):
                S[u, b, :, 0:half] = got[rows * b : rows * (b + 1)].astype(BF16)
                S[u, b, :, half:T] = got[rows * (b + 4) : rows * (b + 5)].astype(BF16)
            end_sends(u)
        refill(t)

    def over(first, last, body):
        def step(i, carry):
            body(i)
            return carry

        lax.fori_loop(first, last, step, 0)

    pl.semaphore_wait(barrier, 8)

    def sk_copy(i):
        return remote(SK.at[i], SKR.at[c], sk_s.at[i], sk_r.at[c], {"col": dest(i)})

    def sk_arrival(j):
        return remote(SK.at[0], SKR.at[j], sk_s.at[0], sk_r.at[j], {"col": other})

    is_copy = remote(ISK, ISR, is_sem.at[0], is_sem.at[1], {"row": 1 - r})

    def g_copy(d):
        return remote(G.at[c], G.at[c], g_s.at[d - 1], g_r.at[c], {"col": lax.rem(c + d, 8)})

    def g_arrival(j):
        return remote(G.at[j], G.at[j], g_s.at[0], g_r.at[j], {"col": other})

    pout_in.wait()
    sketch = lax.dot_general(gb[...], pout[...], NT_DIMS, preferred_element_type=F32)
    blank = jnp.zeros((rows, 128 - kr), F32)
    for i in range(8):
        SK[i] = jnp.concatenate([sketch[rows * i : rows * (i + 1)], blank], axis=1).astype(BF16)
        if i < 4:
            @pl.when(z != i)
            def _():
                sk_copy(i).start()
        else:
            sk_copy(i).start()
    over(0, 1, y_tile)
    over(1, 1 + nzt, z_tile)

    hid_in.wait()
    pin_in.wait()
    part = jnp.zeros((rows, kr), F32)
    for k in range(ff // T):
        part += lax.dot_general(
            hid[:, k * T : (k + 1) * T], pin[:, k * T : (k + 1) * T], NT_DIMS, preferred_element_type=F32
        )
    ISK[...] = jnp.concatenate([blank, part], axis=1)
    is_copy.start()

    over(1 + nzt, early, y_tile)

    total = SK[z].astype(F32)
    for d in range(1, 8):
        j = lax.rem(c + d, 8)
        sk_arrival(j).wait_recv()
        total += SKR[j].astype(F32)
    is_copy.wait_recv()
    G[c] = (total + (ISK[...] + ISR[...])).astype(BF16)
    for d in range(1, 8):
        g_copy(d).start()

    over(early, nt, y_tile)

    for d in range(1, 8):
        g_arrival(lax.rem(c + d, 8)).wait_recv()
    both = jnp.concatenate([G[j].astype(F32) for j in range(8)], axis=0).astype(BF16)
    eye = (
        lax.broadcasted_iota(jnp.int32, (kr, 128), 0) == lax.broadcasted_iota(jnp.int32, (kr, 128), 1)
    ).astype(F32).astype(BF16)
    turned = lax.dot_general(eye, both, NT_DIMS, preferred_element_type=F32)
    place = lax.broadcasted_iota(jnp.int32, turned.shape, 1)
    start = jnp.int32(0)
    for s in range(docs_ref.shape[0]):
        stop = start + doc_ref[s]
        mine = jnp.where((place >= start) & (place < stop), turned, 0.0).astype(BF16)
        docs_ref[s] = jnp.dot(mine, both, preferred_element_type=F32)[:, kr : 2 * kr]
        start = stop

    def y_stage(u):
        k = u - nz
        y_copy(k).wait_recv()
        for b in range(4):
            S[u, b] = add(S[u, b], YR[k, b])
        end_sends(u)

    def second(u):
        @pl.when(z == 1)
        def _():
            zr_copy(u, 1).wait_recv()
            for b in (2, 3):
                S[u, b] = add(S[u, b], RR[u, b - 1])
            zr_copy(u, 2).start()

        @pl.when(z == 2)
        def _():
            zl_copy(u, 3).wait_recv()
            for b in (0, 1):
                S[u, b] = add(S[u, b], RL[u, b])
            zl_copy(u, 2).start()

    def third(u):
        @pl.when(z == 2)
        def _():
            zr_copy(u, 2).wait_recv()
            S[u, 3] = add(S[u, 3], RR[u, 2])
            zr_copy(u, 3).start()

        @pl.when(z == 1)
        def _():
            zl_copy(u, 2).wait_recv()
            S[u, 0] = add(S[u, 0], RL[u, 0])
            zl_copy(u, 1).start()

    def store(u, value):
        @pl.when(u < nz)
        def _():
            FO[u] = value[:, 0:half].astype(BF16)
            FS[u] = value[:, half:T].astype(BF16)
            f_copy(u).start()

        @pl.when(u >= nz)
        def _():
            k = u - nz
            t = jnp.where(k == 0, 0, k + nzt)
            og_ref[:, pl.ds(pl.multiple_of(t * T, T), T)] = value.astype(BF16)

    def last(u):
        @pl.when(z == 0)
        def _():
            zl_copy(u, 1).wait_recv()
            store(u, S[u, 0].astype(F32) + RL[u, 0].astype(F32))

        @pl.when(z == 3)
        def _():
            zr_copy(u, 3).wait_recv()
            store(u, S[u, 3].astype(F32) + RR[u, 2].astype(F32))

        @pl.when(z == 1)
        def _():
            store(u, S[u, 1].astype(F32) + RR[u, 0].astype(F32) + RL[u, 1].astype(F32))

        @pl.when(z == 2)
        def _():
            store(u, S[u, 2].astype(F32) + RR[u, 1].astype(F32) + RL[u, 2].astype(F32))

    def fold(u):
        f_copy(u).wait_recv()
        og_ref[:, pl.ds(pl.multiple_of(T + u * half, half), half)] = add(FO[u], FR[u])

    def at_lag(i, stages, body):
        u = i - stages * lag

        @pl.when((u >= 0) & (u < nu))
        def _():
            body(u)

    def step(i):
        @pl.when((i >= nz) & (i < nu))
        def _():
            y_stage(i)

        at_lag(i, 1, second)
        at_lag(i, 2, third)
        at_lag(i, 3, last)

    over(0, nu + 3 * lag, step)
    over(0, nz, fold)

    def sent_y(k):
        y_copy(k).wait_send()

    def sent_f(u):
        f_copy(u).wait_send()

    def sent_z(u):
        for at in range(4):
            @pl.when(z == at)
            def _():
                if at < 3:
                    zr_copy(u, at + 1).wait_send()
                if at > 0:
                    zl_copy(u, at).wait_send()

    over(0, ny, sent_y)
    over(0, nz, sent_f)
    over(0, nu, sent_z)
    for i in range(8):
        if i < 4:
            @pl.when(z != i)
            def _():
                sk_copy(i).wait_send()
        else:
            sk_copy(i).wait_send()
    is_copy.wait_send()
    for d in range(1, 8):
        g_copy(d).wait_send()


def fused(grad_out, hidden, weight, proj_in, proj_out, doc_len, T=512, wbufs=4, lag=3):
    tokens, depth = grad_out.shape
    rows, ff = hidden.shape
    kr = proj_in.shape[0]
    docs = doc_len.shape[0]
    nt = ff // T
    nzt = max(1, (2 * nt + 6) // 13)
    nz, ny = 2 * nzt, nt - nzt
    nu = nz + ny
    dma = pltpu.SemaphoreType.DMA
    any_spec = pl.BlockSpec(memory_space=pl.ANY)
    vmem_spec = pl.BlockSpec(memory_space=pltpu.VMEM)
    return pl.pallas_call(
        functools.partial(kernel, T, nt, nzt, wbufs, lag),
        out_shape=(
            jax.ShapeDtypeStruct((rows, ff), BF16),
            jax.ShapeDtypeStruct((docs, kr, kr), F32),
        ),
        in_specs=[pl.BlockSpec(memory_space=pltpu.SMEM)] + [any_spec] * 5,
        out_specs=(vmem_spec, vmem_spec),
        scratch_shapes=[
            pltpu.VMEM((8, rows, depth), BF16),
            pltpu.VMEM((tokens, depth), F32),
            pltpu.VMEM((tokens, depth), BF16),
            pltpu.VMEM((rows, ff), BF16),
            pltpu.VMEM((kr, ff), BF16),
            pltpu.VMEM((kr, depth), BF16),
            pltpu.VMEM((wbufs, depth, T), BF16),
            pltpu.VMEM((nu, 4, rows, T), BF16),
            pltpu.VMEM((ny, 4, rows, T), BF16),
            pltpu.VMEM((ny, 4, rows, T), BF16),
            pltpu.VMEM((nu, 3, rows, T), BF16),
            pltpu.VMEM((nu, 3, rows, T), BF16),
            pltpu.VMEM((nz, rows, T // 2), BF16),
            pltpu.VMEM((nz, rows, T // 2), BF16),
            pltpu.VMEM((nz, rows, T // 2), BF16),
            pltpu.VMEM((8, rows, 128), BF16),
            pltpu.VMEM((8, rows, 128), BF16),
            pltpu.VMEM((rows, 128), F32),
            pltpu.VMEM((rows, 128), F32),
            pltpu.VMEM((8, rows, 128), BF16),
            dma((11,)),
            dma((wbufs,)),
            dma((ny,)), dma((ny,)),
            dma((nu,)), dma((nu,)), dma((nu,)), dma((nu,)),
            dma((nz,)), dma((nz,)),
            dma((8,)), dma((8,)), dma((2,)), dma((7,)), dma((8,)),
        ],
        compiler_params=pltpu.CompilerParams(
            collective_id=0, has_side_effects=True, vmem_limit_bytes=60 * 1024 * 1024
        ),
        cost_estimate=pl.CostEstimate(
            flops=2 * tokens * depth * ff, bytes_accessed=2 * depth * ff, transcendentals=0
        ),
    )(doc_len, grad_out.reshape(8, rows, depth), hidden, weight, proj_in, proj_out)


def solution(mesh):
    in_specs = (
        P("grp", "col"),
        P(("grp", "col"), "row"),
        P("col", "row"),
        P(None, "row"),
        P(None, "col"),
        P("grp"),
    )
    out_specs = (P(("grp", "col"), "row"), P("grp", None, None))
    body = fused if mesh.shape["col"] == 8 and mesh.shape["row"] == 2 else local
    return jax.shard_map(body, mesh=mesh, in_specs=in_specs, out_specs=out_specs, check_vma=False)
```

```python
import functools

import jax
import jax.numpy as jnp
from jax import lax
from jax.experimental import pallas as pl
from jax.experimental.pallas import tpu as pltpu
from jax.sharding import PartitionSpec as P

MESH = pl.DeviceIdType.MESH
F32, BF16 = jnp.float32, jnp.bfloat16
NT_DIMS = (((1,), (1,)), ((), ()))


def member_table(doc_len, first, count):
    starts = jnp.cumsum(doc_len) - doc_len
    places = first + jnp.arange(count, dtype=jnp.int32)
    member = (places[None, :] >= starts[:, None]) & (places[None, :] < (starts + doc_len)[:, None])
    return member.astype(jnp.float32)


def doc_terms(doc_len, first, out_part, in_part):
    member = member_table(doc_len, first, out_part.shape[0])
    weighted = member[:, :, None] * out_part.astype(jnp.float32)[None, :, :]
    return jnp.einsum("sti,tj->sij", weighted, in_part.astype(jnp.float32))


def local(grad_out, hidden, weight, proj_in, proj_out, doc_len):
    contract = (((1,), (1,)), ((), ()))
    local_rows = hidden.shape[0]
    local_in = lax.dot_general(hidden, proj_in, contract, preferred_element_type=jnp.float32)
    in_sketch = lax.psum(local_in, "row").astype(jnp.bfloat16)
    input_grad = lax.psum_scatter(
        jnp.dot(grad_out, weight, preferred_element_type=jnp.float32).astype(jnp.bfloat16),
        "col",
        scatter_dimension=0,
        tiled=True,
    )
    local_out = lax.dot_general(grad_out, proj_out, contract, preferred_element_type=jnp.float32)
    out_sketch = lax.psum_scatter(
        local_out.astype(jnp.bfloat16), "col", scatter_dimension=0, tiled=True
    )
    first = lax.axis_index("col") * local_rows
    local_docs = doc_terms(doc_len, first, out_sketch, in_sketch)
    doc_grads = lax.psum(local_docs.astype(jnp.bfloat16), "col").astype(jnp.float32)
    return (input_grad, doc_grads)


def add(a, b):
    return (a.astype(F32) + b.astype(F32)).astype(BF16)


def kernel(
    T, nt, nzt, wbufs, lag,
    doc_ref, grad_hbm, hid_hbm, w_hbm, pin_hbm, pout_hbm,
    og_ref, docs_ref,
    gp, gf, gb, hid, pin, pout, wb,
    S, Q, YR, RR, RL, FO, FS, FR,
    SK, SKR, ISK, ISR, G,
    ld_sem, w_sem,
    y_s, y_r, zr_s, zr_r, zl_s, zl_r, f_s, f_r,
    sk_s, sk_r, is_sem, g_s, g_r,
):
    nz, ny = 2 * nzt, nt - nzt
    nu = nz + ny
    early = min(3 + nzt, nt)
    half = T // 2
    rows = gp.shape[1]
    kr = pout.shape[0]
    ff = hid.shape[1]

    c = lax.axis_index("col")
    r = lax.axis_index("row")
    y, z = lax.rem(c, 2), lax.div(c, 2)
    other = c + 1 - 2 * y
    right, left = lax.rem(c + 2, 8), lax.rem(c + 6, 8)

    def dest(i):
        return 2 * (i % 4) + (y if i < 4 else 1 - y)

    grad_in = [pltpu.make_async_copy(grad_hbm.at[dest(i)], gp.at[i], ld_sem.at[i]) for i in range(8)]
    for cp in grad_in:
        cp.start()

    def w_copy(t):
        return pltpu.make_async_copy(
            w_hbm.at[:, pl.ds(pl.multiple_of(t * T, T), T)], wb.at[lax.rem(t, wbufs)], w_sem.at[lax.rem(t, wbufs)]
        )

    w_copy(jnp.int32(0)).start()
    pout_in = pltpu.make_async_copy(pout_hbm, pout, ld_sem.at[8])
    pin_in = pltpu.make_async_copy(pin_hbm, pin, ld_sem.at[9])
    hid_in = pltpu.make_async_copy(hid_hbm, hid, ld_sem.at[10])
    for t in range(1, wbufs):
        w_copy(jnp.int32(t)).start()
    pout_in.start()
    hid_in.start()
    pin_in.start()

    barrier = pltpu.get_barrier_semaphore()
    for d in range(1, 8):
        pl.semaphore_signal(barrier, inc=1, device_id={"col": lax.rem(c + d, 8)}, device_id_type=MESH)
    pl.semaphore_signal(barrier, inc=1, device_id={"row": 1 - r}, device_id_type=MESH)

    def remote(src, dst, s, rcv, to):
        return pltpu.make_async_remote_copy(
            src_ref=src, dst_ref=dst, send_sem=s, recv_sem=rcv, device_id=to, device_id_type=MESH
        )

    def y_copy(k):
        return remote(Q.at[k], YR.at[k], y_s.at[k], y_r.at[k], {"col": other})

    def zr_copy(u, lo):
        return remote(S.at[u, lo:4], RR.at[u, lo - 1 : 3], zr_s.at[u], zr_r.at[u], {"col": right})

    def zl_copy(u, hi):
        return remote(S.at[u, 0:hi], RL.at[u, 0:hi], zl_s.at[u], zl_r.at[u], {"col": left})

    def f_copy(u):
        return remote(FS.at[u], FR.at[u], f_s.at[u], f_r.at[u], {"col": other})

    def end_sends(u):
        @pl.when(z == 0)
        def _():
            zr_copy(u, 1).start()

        @pl.when(z == 3)
        def _():
            zl_copy(u, 3).start()

    for cp in grad_in:
        cp.wait()
    for i in range(8):
        gf[rows * i : rows * (i + 1), :] = gp[i].astype(F32)
    gb[...] = gf[...].astype(BF16)

    def product(slot, at):
        return jnp.dot(gb[...], wb[slot, :, at : at + half], preferred_element_type=F32)

    def refill(t):
        @pl.when(t + wbufs < nt)
        def _():
            w_copy(t + wbufs).start()

    def y_tile(t):
        k = jnp.where(t == 0, 0, t - nzt)
        w_copy(t).wait()
        slot = lax.rem(t, wbufs)
        for n in range(2):
            got = product(slot, n * half)
            for b in range(4):
                S[nz + k, b, :, n * half : (n + 1) * half] = got[rows * b : rows * (b + 1)].astype(BF16)
                Q[k, b, :, n * half : (n + 1) * half] = got[rows * (b + 4) : rows * (b + 5)].astype(BF16)
        refill(t)
        y_copy(k).start()

    def z_tile(t):
        w_copy(t).wait()
        slot = lax.rem(t, wbufs)
        for n in range(2):
            u = 2 * (t - 1) + n
            got = product(slot, n * half)
            for b in range(4):
                S[u, b, :, 0:half] = got[rows * b : rows * (b + 1)].astype(BF16)
                S[u, b, :, half:T] = got[rows * (b + 4) : rows * (b + 5)].astype(BF16)
            end_sends(u)
        refill(t)

    def over(first, last, body):
        def step(i, carry):
            body(i)
            return carry

        lax.fori_loop(first, last, step, 0)

    pl.semaphore_wait(barrier, 8)

    def sk_copy(i):
        return remote(SK.at[i], SKR.at[c], sk_s.at[i], sk_r.at[c], {"col": dest(i)})

    def sk_arrival(j):
        return remote(SK.at[0], SKR.at[j], sk_s.at[0], sk_r.at[j], {"col": other})

    is_copy = remote(ISK, ISR, is_sem.at[0], is_sem.at[1], {"row": 1 - r})

    def g_copy(d):
        return remote(G.at[c], G.at[c], g_s.at[d - 1], g_r.at[c], {"col": lax.rem(c + d, 8)})

    def g_arrival(j):
        return remote(G.at[j], G.at[j], g_s.at[0], g_r.at[j], {"col": other})

    pout_in.wait()
    sketch = lax.dot_general(gb[...], pout[...], NT_DIMS, preferred_element_type=F32)
    blank = jnp.zeros((rows, 128 - kr), F32)
    for i in range(8):
        SK[i] = jnp.concatenate([sketch[rows * i : rows * (i + 1)], blank], axis=1).astype(BF16)
        if i < 4:
            @pl.when(z != i)
            def _():
                sk_copy(i).start()
        else:
            sk_copy(i).start()
    over(0, 1, y_tile)
    over(1, 1 + nzt, z_tile)

    hid_in.wait()
    pin_in.wait()
    part = jnp.zeros((rows, kr), F32)
    for k in range(ff // T):
        part += lax.dot_general(
            hid[:, k * T : (k + 1) * T], pin[:, k * T : (k + 1) * T], NT_DIMS, preferred_element_type=F32
        )
    ISK[...] = jnp.concatenate([blank, part], axis=1)
    is_copy.start()

    over(1 + nzt, early, y_tile)

    total = SK[z].astype(F32)
    for d in range(1, 8):
        j = lax.rem(c + d, 8)
        sk_arrival(j).wait_recv()
        total += SKR[j].astype(F32)
    is_copy.wait_recv()
    G[c] = (total + (ISK[...] + ISR[...])).astype(BF16)
    for d in range(1, 8):
        g_copy(d).start()

    over(early, nt, y_tile)

    for d in range(1, 8):
        g_arrival(lax.rem(c + d, 8)).wait_recv()
    both = jnp.concatenate([G[j].astype(F32) for j in range(8)], axis=0).astype(BF16)
    eye = (
        lax.broadcasted_iota(jnp.int32, (kr, 128), 0) == lax.broadcasted_iota(jnp.int32, (kr, 128), 1)
    ).astype(F32).astype(BF16)
    turned = lax.dot_general(eye, both, NT_DIMS, preferred_element_type=F32)
    place = lax.broadcasted_iota(jnp.int32, turned.shape, 1)
    start = jnp.int32(0)
    for s in range(docs_ref.shape[0]):
        stop = start + doc_ref[s]
        mine = jnp.where((place >= start) & (place < stop), turned, 0.0).astype(BF16)
        docs_ref[s] = jnp.dot(mine, both, preferred_element_type=F32)[:, kr : 2 * kr]
        start = stop

    def y_stage(u):
        k = u - nz
        y_copy(k).wait_recv()
        for b in range(4):
            S[u, b] = add(S[u, b], YR[k, b])
        end_sends(u)

    def second(u):
        @pl.when(z == 1)
        def _():
            zr_copy(u, 1).wait_recv()
            for b in (2, 3):
                S[u, b] = add(S[u, b], RR[u, b - 1])
            zr_copy(u, 2).start()

        @pl.when(z == 2)
        def _():
            zl_copy(u, 3).wait_recv()
            for b in (0, 1):
                S[u, b] = add(S[u, b], RL[u, b])
            zl_copy(u, 2).start()

    def third(u):
        @pl.when(z == 2)
        def _():
            zr_copy(u, 2).wait_recv()
            S[u, 3] = add(S[u, 3], RR[u, 2])
            zr_copy(u, 3).start()

        @pl.when(z == 1)
        def _():
            zl_copy(u, 2).wait_recv()
            S[u, 0] = add(S[u, 0], RL[u, 0])
            zl_copy(u, 1).start()

    def store(u, value):
        @pl.when(u < nz)
        def _():
            FO[u] = value[:, 0:half].astype(BF16)
            FS[u] = value[:, half:T].astype(BF16)
            f_copy(u).start()

        @pl.when(u >= nz)
        def _():
            k = u - nz
            t = jnp.where(k == 0, 0, k + nzt)
            og_ref[:, pl.ds(pl.multiple_of(t * T, T), T)] = value.astype(BF16)

    def last(u):
        @pl.when(z == 0)
        def _():
            zl_copy(u, 1).wait_recv()
            store(u, S[u, 0].astype(F32) + RL[u, 0].astype(F32))

        @pl.when(z == 3)
        def _():
            zr_copy(u, 3).wait_recv()
            store(u, S[u, 3].astype(F32) + RR[u, 2].astype(F32))

        @pl.when(z == 1)
        def _():
            store(u, S[u, 1].astype(F32) + RR[u, 0].astype(F32) + RL[u, 1].astype(F32))

        @pl.when(z == 2)
        def _():
            store(u, S[u, 2].astype(F32) + RR[u, 1].astype(F32) + RL[u, 2].astype(F32))

    def fold(u):
        f_copy(u).wait_recv()
        og_ref[:, pl.ds(pl.multiple_of(T + u * half, half), half)] = add(FO[u], FR[u])

    def at_lag(i, stages, body):
        u = i - stages * lag

        @pl.when((u >= 0) & (u < nu))
        def _():
            body(u)

    def step(i):
        @pl.when((i >= nz) & (i < nu))
        def _():
            y_stage(i)

        at_lag(i, 1, second)
        at_lag(i, 2, third)
        at_lag(i, 3, last)

    over(0, nu + 3 * lag, step)
    over(0, nz, fold)

    def sent_y(k):
        y_copy(k).wait_send()

    def sent_f(u):
        f_copy(u).wait_send()

    def sent_z(u):
        for at in range(4):
            @pl.when(z == at)
            def _():
                if at < 3:
                    zr_copy(u, at + 1).wait_send()
                if at > 0:
                    zl_copy(u, at).wait_send()

    over(0, ny, sent_y)
    over(0, nz, sent_f)
    over(0, nu, sent_z)
    for i in range(8):
        if i < 4:
            @pl.when(z != i)
            def _():
                sk_copy(i).wait_send()
        else:
            sk_copy(i).wait_send()
    is_copy.wait_send()
    for d in range(1, 8):
        g_copy(d).wait_send()


def settle(a, b, a_out, b_out, sem):
    first = pltpu.make_async_copy(a, a_out, sem.at[0])
    second = pltpu.make_async_copy(b, b_out, sem.at[1])
    first.start()
    second.start()
    first.wait()
    second.wait()


def fused(grad_out, hidden, weight, proj_in, proj_out, doc_len, T=512, wbufs=4, lag=3):
    tokens, depth = grad_out.shape
    rows, ff = hidden.shape
    kr = proj_in.shape[0]
    docs = doc_len.shape[0]
    nt = ff // T
    nzt = max(1, (2 * nt + 6) // 13)
    nz, ny = 2 * nzt, nt - nzt
    nu = nz + ny
    dma = pltpu.SemaphoreType.DMA
    any_spec = pl.BlockSpec(memory_space=pl.ANY)
    vmem_spec = pl.BlockSpec(memory_space=pltpu.VMEM)
    shapes = (
        jax.ShapeDtypeStruct((rows, ff), BF16),
        jax.ShapeDtypeStruct((docs, kr, kr), F32),
    )
    made = pl.pallas_call(
        functools.partial(kernel, T, nt, nzt, wbufs, lag),
        out_shape=shapes,
        in_specs=[pl.BlockSpec(memory_space=pltpu.SMEM)] + [any_spec] * 5,
        out_specs=(vmem_spec, vmem_spec),
        scratch_shapes=[
            pltpu.VMEM((8, rows, depth), BF16),
            pltpu.VMEM((tokens, depth), F32),
            pltpu.VMEM((tokens, depth), BF16),
            pltpu.VMEM((rows, ff), BF16),
            pltpu.VMEM((kr, ff), BF16),
            pltpu.VMEM((kr, depth), BF16),
            pltpu.VMEM((wbufs, depth, T), BF16),
            pltpu.VMEM((nu, 4, rows, T), BF16),
            pltpu.VMEM((ny, 4, rows, T), BF16),
            pltpu.VMEM((ny, 4, rows, T), BF16),
            pltpu.VMEM((nu, 3, rows, T), BF16),
            pltpu.VMEM((nu, 3, rows, T), BF16),
            pltpu.VMEM((nz, rows, T // 2), BF16),
            pltpu.VMEM((nz, rows, T // 2), BF16),
            pltpu.VMEM((nz, rows, T // 2), BF16),
            pltpu.VMEM((8, rows, 128), BF16),
            pltpu.VMEM((8, rows, 128), BF16),
            pltpu.VMEM((rows, 128), F32),
            pltpu.VMEM((rows, 128), F32),
            pltpu.VMEM((8, rows, 128), BF16),
            dma((11,)),
            dma((wbufs,)),
            dma((ny,)), dma((ny,)),
            dma((nu,)), dma((nu,)), dma((nu,)), dma((nu,)),
            dma((nz,)), dma((nz,)),
            dma((8,)), dma((8,)), dma((2,)), dma((7,)), dma((8,)),
        ],
        compiler_params=pltpu.CompilerParams(
            collective_id=0, has_side_effects=True, vmem_limit_bytes=60 * 1024 * 1024
        ),
        cost_estimate=pl.CostEstimate(
            flops=2 * tokens * depth * ff, bytes_accessed=2 * depth * ff, transcendentals=0
        ),
    )(doc_len, grad_out.reshape(8, rows, depth), hidden, weight, proj_in, proj_out)
    return pl.pallas_call(
        settle,
        out_shape=shapes,
        in_specs=[vmem_spec] * 2,
        out_specs=(any_spec, any_spec),
        scratch_shapes=[dma((2,))],
    )(*made)


def solution(mesh):
    in_specs = (
        P("grp", "col"),
        P(("grp", "col"), "row"),
        P("col", "row"),
        P(None, "row"),
        P(None, "col"),
        P("grp"),
    )
    out_specs = (P(("grp", "col"), "row"), P("grp", None, None))
    body = fused if mesh.shape["col"] == 8 and mesh.shape["row"] == 2 else local
    return jax.shard_map(body, mesh=mesh, in_specs=in_specs, out_specs=out_specs, check_vma=False)
```
